32 devices in a mesh: space: 8 (over z, core), vel: 4 (over y, x).
Axes of the slice: x: 2, y: 2, z: 4, core: 2. Of those that a mesh axis runs over, the one named last changes fastest.
Arguments:
- distribution: float32 [64, 4, 4, 2, 16384], P('space', None, None, None, 'vel'), may hold values from 0 to 15, as said below
Outputs:
- evolved: float32 [64, 4, 4, 2, 16384], P('space', None, None, None, 'vel')
The draws below stay inside these ranges and needn't reach their ends.
Inputs may be any that keep to these rules, and one draw needn't show every extreme that they name: `distribution`: every entry is non-negative.
All inputs are finite; a program needn't handle non-finite values.
Results may differ from the reference program's by a relative error of at most 0.0001.
Values sent between devices are 32-bit elements; how exact they have to be, the bound alone decides.
A program may use at most 64 MiB of HBM per device.

```python
import math
import jax
import jax.numpy as jnp
from jax import lax

NV = 32
NVH = 16384
NY = 4
NZ = 4
STEPS = 3
NX = 64


speed_limit = 8.0


def draw_distribution(key, part):
    keys = jax.random.split(key, 8)
    cells = (NX, NY, NZ)
    dense_main = jax.random.uniform(keys[0], cells, jnp.float32, 0.4, 1.2)
    dense_beam = jax.random.uniform(keys[1], cells, jnp.float32, 0.1, 0.6)
    heat_main = jnp.exp(jax.random.uniform(keys[2], cells, jnp.float32, math.log(0.6), math.log(1.6)))
    heat_beam = jnp.exp(jax.random.uniform(keys[3], cells, jnp.float32, math.log(0.6), math.log(1.6)))
    drift_main = jax.random.uniform(keys[4], (3, NX, NY, NZ), jnp.float32, -0.6, 0.6)
    boost = jnp.array([1.5, 0.0, 0.0], jnp.float32)[:, None, None, None]
    drift_beam = drift_main + boost + jax.random.uniform(keys[5], (3, NX, NY, NZ), jnp.float32, -0.3, 0.3)
    factor = jnp.exp(jax.random.uniform(keys[6], (NX, NY, NZ, 2, NVH), jnp.float32, -1.15, 1.15))
    spacing = 2.0 * speed_limit / NV
    flat_index = jnp.arange(NVH, dtype=jnp.int32)
    xlevel = (flat_index // (NV * NV)).astype(jnp.float32)
    ylevel = (flat_index // NV % NV).astype(jnp.float32)
    zlevel = (flat_index % NV).astype(jnp.float32)
    direction = (2 * jnp.arange(2, dtype=jnp.int32) - 1).astype(jnp.float32)[:, None]
    xspeed = direction * ((xlevel + 0.5) * spacing)[None, :]
    yspeed = (-speed_limit + (ylevel + 0.5) * spacing)[None, :]
    zspeed = (-speed_limit + (zlevel + 0.5) * spacing)[None, :]

    def maxwellian(dense, heat, drift):

        def cell(values):
            return values[..., None, None]
        square = (xspeed - cell(drift[0])) ** 2 + (yspeed - cell(drift[1])) ** 2 + (zspeed - cell(drift[2])) ** 2
        return cell(dense) * cell(heat) ** (-1.5) * jnp.exp(-0.5 * square / cell(heat))
    return factor * (maxwellian(dense_main, heat_main, drift_main) + maxwellian(dense_beam, heat_beam, drift_beam))


def setup_inputs(seed: int = 0) -> dict:
    seeds = jax.random.split(jax.random.key(seed), 2)
    distribution = draw_distribution(jax.random.fold_in(seeds[1], 71), 0)
    return dict(distribution=distribution)


speed_limit = 8.0
courant = 1.9
diffusivity_ratio = 2.0 / 3.0
encounter_rate = 0.7
shear_power_index = 0.75


def velocity_table(offset, velocities):
    spacing = 2.0 * speed_limit / NV
    flat_index = offset + jnp.arange(velocities, dtype=jnp.int32)
    xlevel = (flat_index // (NV * NV)).astype(jnp.float32)
    ylevel = ((flat_index // NV) % NV).astype(jnp.float32)
    zlevel = (flat_index % NV).astype(jnp.float32)
    direction = (2 * jnp.arange(2, dtype=jnp.int32) - 1).astype(jnp.float32)[:, None]
    xspeed = direction * ((xlevel + 0.5) * spacing)[None, :]
    yspeed = jnp.broadcast_to((-speed_limit + (ylevel + 0.5) * spacing)[None, :], xspeed.shape)
    zspeed = jnp.broadcast_to((-speed_limit + (zlevel + 0.5) * spacing)[None, :], xspeed.shape)
    return xspeed, yspeed, zspeed


def moment_weights(xspeed, yspeed, zspeed):
    spacing = 2.0 * speed_limit / NV
    quadrature = spacing ** 3 / (2.0 * math.pi) ** 1.5
    square = xspeed * xspeed + yspeed * yspeed + zspeed * zspeed
    rows = [jnp.ones_like(xspeed), xspeed, yspeed, zspeed, xspeed * xspeed, yspeed * yspeed,
            zspeed * zspeed, xspeed * yspeed, xspeed * zspeed, yspeed * zspeed,
            xspeed * square, yspeed * square, zspeed * square]
    return quadrature * jnp.stack(rows)


def moments_of(current, weights):
    flat = current.reshape(-1, weights.shape[1] * weights.shape[2])
    table = weights.reshape(weights.shape[0], -1)
    return lax.dot_general(table, flat, (((1,), (1,)), ((), ())),
                           precision=lax.Precision.HIGHEST, preferred_element_type=jnp.float32)


def cell_fields(moments):
    matter_concentration = moments[0]
    impulse_first_axis = moments[1] / matter_concentration
    impulse_second_axis = moments[2] / matter_concentration
    impulse_third_axis = moments[3] / matter_concentration
    whole_internal_work = moments[4] + moments[5] + moments[6]
    velocity_norm_power = impulse_first_axis * impulse_first_axis + impulse_second_axis * impulse_second_axis + impulse_third_axis * impulse_third_axis
    thermal_state = (whole_internal_work / matter_concentration - velocity_norm_power) / 3.0
    along_flow = impulse_first_axis * moments[1] + impulse_second_axis * moments[2] + impulse_third_axis * moments[3]
    xheating = 0.5 * (moments[10] - 2.0 * (impulse_first_axis * moments[4] + impulse_second_axis * moments[7] + impulse_third_axis * moments[8])
                      - impulse_first_axis * whole_internal_work + velocity_norm_power * moments[1] + 2.0 * impulse_first_axis * along_flow
                      - impulse_first_axis * velocity_norm_power * matter_concentration)
    yheating = 0.5 * (moments[11] - 2.0 * (impulse_first_axis * moments[7] + impulse_second_axis * moments[5] + impulse_third_axis * moments[9])
                      - impulse_second_axis * whole_internal_work + velocity_norm_power * moments[2] + 2.0 * impulse_second_axis * along_flow
                      - impulse_second_axis * velocity_norm_power * matter_concentration)
    zheating = 0.5 * (moments[12] - 2.0 * (impulse_first_axis * moments[8] + impulse_second_axis * moments[9] + impulse_third_axis * moments[6])
                      - impulse_third_axis * whole_internal_work + velocity_norm_power * moments[3] + 2.0 * impulse_third_axis * along_flow
                      - impulse_third_axis * velocity_norm_power * matter_concentration)
    normal_stress_level = matter_concentration * thermal_state
    conduction_factor = (1.0 - diffusivity_ratio) / (5.0 * normal_stress_level * thermal_state)
    perturbation_height = matter_concentration * thermal_state ** -1.5
    surviving_share = jnp.exp(-encounter_rate * matter_concentration * thermal_state ** (1.0 - shear_power_index))
    return jnp.stack([perturbation_height, impulse_first_axis, impulse_second_axis, impulse_third_axis, 1.0 / thermal_state,
                      conduction_factor * xheating, conduction_factor * yheating, conduction_factor * zheating, surviving_share])


def collide(current, fields, xspeed, yspeed, zspeed):
    def field(which):
        return fields[which][..., None, None]
    xdrift = xspeed - field(1)
    ydrift = yspeed - field(2)
    zdrift = zspeed - field(3)
    energy = (xdrift * xdrift + ydrift * ydrift + zdrift * zdrift) * field(4)
    heat_term = xdrift * field(5) + ydrift * field(6) + zdrift * field(7)
    target = field(0) * jnp.exp(-0.5 * energy) * (1.0 + heat_term * (energy - 5.0))
    return target + (current - target) * field(8)


def sweep_shares(speed):
    courant_ratio = courant / ((NV - 1) * speed_limit / NV)
    fraction = courant_ratio * jnp.abs(speed)
    own_share = (1.0 - fraction) * (1.0 - 0.5 * fraction)
    near_share = fraction * (2.0 - fraction)
    far_share = 0.5 * fraction * (fraction - 1.0)
    forward = speed > 0.0
    nothing = jnp.zeros_like(speed)
    return (own_share, jnp.where(forward, near_share, nothing), jnp.where(forward, far_share, nothing),
            jnp.where(forward, nothing, near_share), jnp.where(forward, nothing, far_share))


def periodic_sweep(current, shares, along):
    own_share, near_back, far_back, near_front, far_front = shares
    return (own_share * current + near_back * jnp.roll(current, 1, along) + far_back * jnp.roll(current, 2, along)
            + near_front * jnp.roll(current, -1, along) + far_front * jnp.roll(current, -2, along))


def reference(distribution):
    xspeed, yspeed, zspeed = velocity_table(0, NVH)
    weights = moment_weights(xspeed, yspeed, zspeed)
    xshares = sweep_shares(xspeed)
    yshares = sweep_shares(yspeed)
    zshares = sweep_shares(zspeed)
    current = distribution
    for repeat in range(STEPS):
        moments = moments_of(current, weights)
        fields = jnp.moveaxis(cell_fields(moments).reshape(9, NX, NY, NZ), 1, 0)

        def collide_plane(pair):
            return collide(pair[0], pair[1], xspeed, yspeed, zspeed)

        relaxed = lax.map(collide_plane, (current, fields))
        padded = jnp.pad(relaxed, ((2, 2), (0, 0), (0, 0), (0, 0), (0, 0)))

        def move_plane(plane):
            window = lax.dynamic_slice_in_dim(padded, plane, 5, 0)
            own_share, near_back, far_back, near_front, far_front = xshares
            moved = (own_share * window[2] + near_back * window[1] + far_back * window[0]
                     + near_front * window[3] + far_front * window[4])
            moved = periodic_sweep(moved, yshares, 0)
            return periodic_sweep(moved, zshares, 1)

        current = lax.map(move_plane, jnp.arange(NX, dtype=jnp.int32))
    return current
```

```python
import functools
import math

import jax
import jax.numpy as jnp
import ml_dtypes
import numpy as np
from jax import lax
from jax.experimental import pallas as pl
from jax.experimental.pallas import tpu as pltpu
from jax.sharding import PartitionSpec as P

NV = 32
STEPS = 3
SUB = 8
LANES = 128

speed_limit = 8.0
courant = 1.9
diffusivity_ratio = 2.0 / 3.0
encounter_rate = 0.7

SPACING = 2.0 * speed_limit / NV
QUADRATURE = SPACING**3 / (2.0 * math.pi) ** 1.5
COURANT_RATIO = courant / ((NV - 1) * speed_limit / NV)
PER_LANES = LANES // NV
MESH = pl.DeviceIdType.MESH
BLOCKS = [(0, 0), (0, 1), (0, 2), (0, 3), (1, 0), (1, 1), (1, 2), (2, 0), (2, 1), (3, 0)]
ROWS = 16


def moment_table():
    lane = np.arange(LANES)
    y = SPACING * (lane // NV - 0.5 * (PER_LANES - 1))
    z = -speed_limit + (lane % NV + 0.5) * SPACING
    one = np.ones(LANES)
    terms = {
        (0, 0): {0: one, 2: y, 3: z, 5: y * y, 6: z * z, 9: y * z, 11: y**3 + y * z * z, 12: z * y * y + z**3},
        (0, 1): {2: one, 5: 2 * y, 9: z, 11: 3 * y * y + z * z, 12: 2 * y * z},
        (0, 2): {5: one, 11: 3 * y, 12: z},
        (0, 3): {11: one},
        (1, 0): {1: one, 7: y, 8: z, 10: y * y + z * z},
        (1, 1): {7: one, 10: 2 * y},
        (1, 2): {10: one},
        (2, 0): {4: one, 11: y, 12: z},
        (2, 1): {11: one},
        (3, 0): {10: one},
    }
    table = np.zeros((len(BLOCKS) * LANES, ROWS))
    for place, block in enumerate(BLOCKS):
        for row, values in terms[block].items():
            table[place * LANES : (place + 1) * LANES, row] = values
    out = np.zeros((len(BLOCKS) * LANES, LANES), ml_dtypes.bfloat16)
    rest = table
    for part in range(3):
        piece = rest.astype(ml_dtypes.bfloat16)
        out[:, part * ROWS : (part + 1) * ROWS] = piece
        rest = rest - piece.astype(np.float64)
    return out


def field_rows(m, xi):
    rho = m[0]
    ux, uy, uz = m[1] / rho, m[2] / rho, m[3] / rho
    work = m[4] + m[5] + m[6]
    norm = ux * ux + uy * uy + uz * uz
    temp = (work / rho - norm) / 3.0
    along = ux * m[1] + uy * m[2] + uz * m[3]

    def heat(third, first, stress, u):
        return 0.5 * (
            third
            - 2.0 * (ux * stress[0] + uy * stress[1] + uz * stress[2])
            - u * work
            + norm * first
            + 2.0 * u * along
            - u * norm * rho
        )

    xheat = heat(m[10], m[1], (m[4], m[7], m[8]), ux)
    yheat = heat(m[11], m[2], (m[7], m[5], m[9]), uy)
    zheat = heat(m[12], m[3], (m[8], m[9], m[6]), uz)
    pressure = rho * temp
    conduct = (1.0 - diffusivity_ratio) / (5.0 * pressure * temp)
    root = jnp.sqrt(temp)
    amp = rho / (temp * root)
    retain = jnp.exp(-encounter_rate * rho * jnp.sqrt(root))
    inv = 1.0 / temp
    drift = xi - ux
    energy = drift * drift * inv
    height = (amp * (1.0 - retain)) * jnp.exp(-0.5 * energy)
    return height, energy - 5.0, drift * (conduct * xheat), [
        uy, uz, inv, conduct * yheat, conduct * zheat, retain,
    ]


def kernel(
    layers, cells, levels, spaces, vels,
    x_ref, w_ref, o_ref,
    stage, g_ref, r_ref, halo, sums, lhs, part, gathered, wide, table, table_halo,
    in_sem, out_sem, halo_send, halo_recv, tab_send, tab_recv, red_send, red_recv,
):
    f32 = jnp.float32
    s = lax.axis_index("space")
    v = lax.axis_index("vel")
    has_up = s < spaces - 1
    has_down = s > 0
    every = layers * cells
    nx = 2 * levels

    edge = 2
    spans = [(0, edge), (layers - edge, edge), (edge, layers - 2 * edge)]
    loads = []
    for i, (first, count) in enumerate(spans):
        rows = pl.ds(first * cells, count * cells)
        copy = pltpu.make_async_copy(x_ref.at[rows], stage.at[rows], in_sem.at[i])
        copy.start()
        loads.append(copy)

    barrier = pltpu.get_barrier_semaphore()
    for off in range(1, vels):
        pl.semaphore_signal(barrier, inc=1, device_id={"vel": lax.rem(v + off, vels)}, device_id_type=MESH)

    @pl.when(has_up)
    def _():
        pl.semaphore_signal(barrier, inc=1, device_id={"space": s + 1}, device_id_type=MESH)

    @pl.when(has_down)
    def _():
        pl.semaphore_signal(barrier, inc=1, device_id={"space": s - 1}, device_id_type=MESH)

    sub = lax.broadcasted_iota(jnp.int32, (SUB, LANES), 0)
    lane = lax.broadcasted_iota(jnp.int32, (SUB, LANES), 1)
    yv = -speed_limit + ((sub * PER_LANES + lane // NV).astype(f32) + 0.5) * SPACING
    zv = -speed_limit + ((lane % NV).astype(f32) + 0.5) * SPACING
    first_level = v * levels

    def speed(a):
        return ((first_level + a).astype(f32) + 0.5) * SPACING

    place = lax.broadcasted_iota(jnp.int32, (nx, every), 0)
    ahead = place >= levels
    level = jnp.where(ahead, place - levels, place) + first_level
    xi = jnp.where(ahead, 1.0, -1.0) * ((level.astype(f32) + 0.5) * SPACING)

    def sweep_coefs(speeds):
        n = COURANT_RATIO * jnp.abs(speeds)
        near = n * (2.0 - n)
        return near, 1.0 - n, jnp.where(speeds > 0.0, -near, near)

    ycoefs = sweep_coefs(yv)
    zcoefs = sweep_coefs(zv)

    def unpack(half, first, count):
        def body(i, _):
            for a in range(levels):
                g_ref[0, half, a, first + i // cells, i % cells] = stage[
                    first * cells + i, pl.ds(a * 2 * SUB + half, SUB, stride=2), :
                ]
            return 0

        lax.fori_loop(0, count * cells, body, 0, unroll=4)

    def stage_one(which, first, count):
        squares = []
        speeds = []
        for a in range(levels):
            xa = speed(jnp.int32(a))
            speeds.append(xa)
            squares.append(xa * xa)

        def body(i, _):
            layer = first + i // cells
            cell = i % cells
            total = [None] * 4
            for a in range(levels):
                back = g_ref[which, 0, a, layer, cell]
                fore = g_ref[which, 1, a, layer, cell]
                even = fore + back
                odd = (fore - back) * speeds[a]
                terms = [even, odd, even * squares[a], odd * squares[a]]
                total = [t if o is None else o + t for o, t in zip(total, terms)]
            at = (layer * cells + cell) * SUB
            for m in range(4):
                sums[m, pl.ds(at, SUB), :] = total[m]
            return 0

        lax.fori_loop(0, count * cells, body, 0, unroll=4)

    def stage_two():
        heights = [2.0 * SPACING * (PER_LANES / 4) * (2 * j - (SUB - 1)) for j in range(SUB)]

        def body(i, _):
            at = pl.multiple_of(i * SUB, SUB)
            for m, powers in enumerate((4, 3, 2, 1)):
                rows = [sums[m, pl.ds(at * SUB + j, SUB, stride=SUB), :] for j in range(SUB)]
                total = [None] * powers
                for j in range(SUB // 2):
                    low, high = rows[j], rows[SUB - 1 - j]
                    size = heights[SUB - 1 - j]
                    even = high + low
                    odd = (high - low) * size if powers > 1 else None
                    terms = [even, odd]
                    if powers > 2:
                        terms.append(even * (size * size))
                    if powers > 3:
                        terms.append(odd * (size * size))
                    total = [t if o is None else o + t for o, t in zip(total, terms[:powers])]
                for p in range(powers):
                    q = BLOCKS.index((m, p))
                    lhs[pl.ds(at, SUB), q * LANES : (q + 1) * LANES] = total[p]
            return 0

        lax.fori_loop(0, every // SUB, body, 0, unroll=2)

    def reduce_copy(k, off):
        return pltpu.make_async_remote_copy(
            src_ref=part.at[k],
            dst_ref=gathered.at[k, off - 1],
            send_sem=red_send.at[k, off - 1],
            recv_sem=red_recv.at[k, off - 1],
            device_id={"vel": lax.rem(v + off, vels)},
            device_id_type=MESH,
        )

    def table_copy(k, half):
        first = (layers - edge) * cells if half else 0
        return pltpu.make_async_remote_copy(
            src_ref=table.at[k, pl.ds(first, edge * cells)],
            dst_ref=table_halo.at[k, half],
            send_sem=tab_send.at[k, half],
            recv_sem=tab_recv.at[k, half],
            device_id={"space": s + 1 if half else s - 1},
            device_id_type=MESH,
        )

    def halo_copy(k, half):
        first = layers - edge if half else 0
        return pltpu.make_async_remote_copy(
            src_ref=g_ref.at[k % 2, half, :, pl.ds(first, edge)],
            dst_ref=halo.at[k, half],
            send_sem=halo_send.at[k, half],
            recv_sem=halo_recv.at[k, half],
            device_id={"space": s + 1 if half else s - 1},
            device_id_type=MESH,
        )

    sends = {0: has_down, 1: has_up}
    receives = {0: has_up, 1: has_down}

    def fields(k):
        stage_two()
        rest = lhs[...]
        acc = None
        for _ in range(3):
            piece = rest.astype(jnp.bfloat16)
            term = jnp.dot(piece, w_ref[...], preferred_element_type=f32)
            acc = term if acc is None else acc + term
            rest = rest - piece.astype(f32)
        turned = acc.T
        part[k] = (turned[0:ROWS] + turned[ROWS : 2 * ROWS] + turned[2 * ROWS : 3 * ROWS]) * QUADRATURE
        for off in range(1, vels):
            reduce_copy(k, off).start()
        total = part[k]
        for off in range(1, vels):
            reduce_copy(k, off).wait_recv()
            total = total + gathered[k, off - 1]
        m = [total[i : i + 1, :] for i in range(13)]
        height, energy, heat, rest = field_rows(m, xi)
        wide[0:nx, :] = height
        wide[nx : 2 * nx, :] = energy
        wide[2 * nx : 3 * nx, :] = heat
        for i, row in enumerate(rest):
            wide[3 * nx + i : 3 * nx + i + 1, :] = row
        table[k] = wide[...].T
        for half in range(2):
            @pl.when(sends[half])
            def _():
                table_copy(k, half).start()

    def relax_cell(row, halves, load, store):
        def spread(i):
            return jnp.broadcast_to(row[:, i : i + 1], (SUB, LANES))

        uy, uz, inv, qy, qz, retain = [spread(3 * nx + i) for i in range(6)]
        cy = yv - uy
        cz = zv - uz
        energy = (cy * cy + cz * cz) * inv
        heat = cy * qy + cz * qz
        gauss = jnp.exp(-0.5 * energy)
        for half in halves:
            for a in range(levels):
                i = half * levels + a
                bracket = 1.0 + (spread(2 * nx + i) + heat) * (spread(nx + i) + energy)
                store(half, a, (spread(i) * gauss) * bracket + load(half, a) * retain)

    def relax_own(k):
        def body(i, _):
            layer = i // cells
            cell = i % cells

            def load(half, a):
                return g_ref[k % 2, half, a, layer, cell]

            def store(half, a, value):
                r_ref[half, a, layer + edge * half, cell] = value

            relax_cell(table[k, pl.ds(i, 1), :], (0, 1), load, store)
            return 0

        lax.fori_loop(0, every, body, 0, unroll=2)

    def relax_halo(k, half):
        def body(i, _):
            layer = i // cells
            cell = i % cells

            def load(half, a):
                return halo[k, half, a, layer, cell]

            def store(half, a, value):
                r_ref[half, a, layer + (0 if half else layers), cell] = value

            relax_cell(table_halo[k, half, pl.ds(i, 1), :], (half,), load, store)
            return 0

        lax.fori_loop(0, edge * cells, body, 0, unroll=2)

    def periodic(values, coefs):
        near, keep, turn = coefs
        even, odd = values[0] + values[2], values[1] + values[3]
        deven, dodd = values[0] - values[2], values[1] - values[3]
        shift = near * (odd - even)
        e, o = even + shift, odd - shift
        de = keep * deven + turn * dodd
        do = keep * dodd - turn * deven
        return [e + de, o + do, e - de, o - do]

    def transport(k, half, first, count):
        last = k == STEPS - 1

        def body(i, _):
            a = i // count
            layer = first + i % count
            n = COURANT_RATIO * speed(a)
            own = 0.25 * (1.0 - n) * (1.0 - 0.5 * n)
            near = 0.25 * n * (2.0 - n)
            far = 0.125 * n * (n - 1.0)
            back = (2, 1, 0) if half else (0, 1, 2)
            moved = []
            for c in range(cells):
                r0, r1, r2 = [r_ref[half, a, layer + b, c] for b in back]
                moved.append(own * r0 + near * r1 + far * r2)
            for z in range(4):
                moved[z::4] = periodic(moved[z::4], ycoefs)
            for y in range(4):
                moved[4 * y : 4 * y + 4] = periodic(moved[4 * y : 4 * y + 4], zcoefs)
            for c in range(cells):
                if last:
                    stage[layer * cells + c, pl.ds(a * 2 * SUB + half, SUB, stride=2), :] = moved[c]
                else:
                    g_ref[(k + 1) % 2, half, a, layer, c] = moved[c]
            return 0

        lax.fori_loop(0, levels * count, body, 0, unroll=2)

    for half in range(2):
        @pl.when(jnp.logical_not(receives[half]))
        def _():
            for a in range(levels):
                for layer in range(edge):
                    r_ref[half, a, layer + (0 if half else layers)] = jnp.zeros((cells, SUB, LANES), f32)

    wide[...] = jnp.zeros_like(wide)

    loads[0].wait()
    unpack(0, 0, edge)
    loads[1].wait()
    unpack(1, layers - edge, edge)

    greeted = vels - 1 + jnp.minimum(s, 1) + jnp.minimum(spaces - 1 - s, 1)
    pl.semaphore_wait(barrier, greeted)

    for half in range(2):
        @pl.when(sends[half])
        def _():
            halo_copy(0, half).start()

    unpack(1, 0, edge)
    unpack(0, layers - edge, edge)
    stage_one(0, 0, edge)
    stage_one(0, layers - edge, edge)
    loads[2].wait()
    unpack(0, edge, layers - 2 * edge)
    unpack(1, edge, layers - 2 * edge)
    stage_one(0, edge, layers - 2 * edge)

    stores = []

    def store_out(i):
        first, count = spans[i]
        rows = pl.ds(first * cells, count * cells)
        copy = pltpu.make_async_copy(stage.at[rows], o_ref.at[rows], out_sem.at[i])
        copy.start()
        stores.append(copy)

    for k in range(STEPS):
        last = k == STEPS - 1
        fields(k)
        relax_own(k)
        transport(k, 1, layers - edge, edge)
        transport(k, 0, 0, edge)
        if not last:
            for half in range(2):
                @pl.when(sends[half])
                def _():
                    halo_copy(k + 1, half).start()
        for half in range(2):
            transport(k, half, edge, layers - 2 * edge)
        if last:
            store_out(2)
        else:
            stage_one((k + 1) % 2, edge, layers - 2 * edge)
        for half in range(2):
            @pl.when(receives[half])
            def _():
                table_copy(k, half).wait_recv()
                halo_copy(k, half).wait_recv()
                relax_halo(k, half)

            transport(k, half, 0 if half else layers - edge, edge)
            span = 0 if half else 1
            if last:
                store_out(span)
            else:
                stage_one((k + 1) % 2, spans[span][0], edge)
        for half in range(2):
            @pl.when(sends[half])
            def _():
                table_copy(k, half).wait_send()
                halo_copy(k, half).wait_send()
        for off in range(1, vels):
            reduce_copy(k, off).wait_send()

    for copy in stores:
        copy.wait()


def local(distribution, weights, spaces, vels):
    layers, breadth, height, halves, velocities = distribution.shape
    cells = breadth * height
    assert breadth == 4 and height == 4 and halves == 2
    levels = velocities // (NV * NV)
    tiles = velocities // LANES
    every = layers * cells
    rows = distribution.reshape(every, halves, tiles, LANES)
    rows = rows.transpose(0, 2, 1, 3).reshape(every, tiles * halves, LANES)
    f32 = jnp.float32
    dma = pltpu.SemaphoreType.DMA
    out = pl.pallas_call(
        functools.partial(kernel, layers, cells, levels, spaces, vels),
        out_shape=jax.ShapeDtypeStruct(rows.shape, f32),
        in_specs=[
            pl.BlockSpec(memory_space=pl.ANY),
            pl.BlockSpec(memory_space=pltpu.VMEM),
        ],
        out_specs=pl.BlockSpec(memory_space=pl.ANY),
        scratch_shapes=[
            pltpu.VMEM(rows.shape, f32),
            pltpu.VMEM((2, 2, levels, layers, cells, SUB, LANES), f32),
            pltpu.VMEM((2, levels, layers + 2, cells, SUB, LANES), f32),
            pltpu.VMEM((STEPS, 2, levels, 2, cells, SUB, LANES), f32),
            pltpu.VMEM((4, every * SUB, LANES), f32),
            pltpu.VMEM((every, len(BLOCKS) * LANES), f32),
            pltpu.VMEM((STEPS, ROWS, every), f32),
            pltpu.VMEM((STEPS, max(vels - 1, 1), ROWS, every), f32),
            pltpu.VMEM((LANES, every), f32),
            pltpu.VMEM((STEPS, every, LANES), f32),
            pltpu.VMEM((STEPS, 2, 2 * cells, LANES), f32),
            dma((3,)),
            dma((3,)),
            dma((STEPS, 2)),
            dma((STEPS, 2)),
            dma((STEPS, 2)),
            dma((STEPS, 2)),
            dma((STEPS, max(vels - 1, 1))),
            dma((STEPS, max(vels - 1, 1))),
        ],
        compiler_params=pltpu.CompilerParams(
            collective_id=0, has_side_effects=True, vmem_limit_bytes=48 * 2**20
        ),
    )(rows, weights)
    out = out.reshape(every, tiles, halves, LANES).transpose(0, 2, 1, 3)
    return out.reshape(distribution.shape)


def solution(mesh):
    weights = moment_table()
    spec = P("space", None, None, None, "vel")
    body = functools.partial(local, spaces=mesh.shape["space"], vels=mesh.shape["vel"])
    mapped = jax.shard_map(
        body, mesh=mesh, in_specs=(spec, P()), out_specs=spec, check_vma=False
    )
    return lambda distribution: mapped(distribution, jnp.asarray(weights))
```

```python
import functools
import math

import jax
import jax.numpy as jnp
import ml_dtypes
import numpy as np
from jax import lax
from jax.experimental import pallas as pl
from jax.experimental.pallas import tpu as pltpu
from jax.sharding import PartitionSpec as P

NV = 32
STEPS = 3
SUB = 8
LANES = 128

speed_limit = 8.0
courant = 1.9
diffusivity_ratio = 2.0 / 3.0
encounter_rate = 0.7

SPACING = 2.0 * speed_limit / NV
QUADRATURE = SPACING**3 / (2.0 * math.pi) ** 1.5
COURANT_RATIO = courant / ((NV - 1) * speed_limit / NV)
PER_LANES = LANES // NV
MESH = pl.DeviceIdType.MESH
BLOCKS = [(0, 0), (0, 1), (0, 2), (0, 3), (1, 0), (1, 1), (1, 2), (2, 0), (2, 1), (3, 0)]
ROWS = 16


def moment_table():
    lane = np.arange(LANES)
    y = SPACING * (lane // NV - 0.5 * (PER_LANES - 1))
    z = -speed_limit + (lane % NV + 0.5) * SPACING
    one = np.ones(LANES)
    terms = {
        (0, 0): {0: one, 2: y, 3: z, 5: y * y, 6: z * z, 9: y * z, 11: y**3 + y * z * z, 12: z * y * y + z**3},
        (0, 1): {2: one, 5: 2 * y, 9: z, 11: 3 * y * y + z * z, 12: 2 * y * z},
        (0, 2): {5: one, 11: 3 * y, 12: z},
        (0, 3): {11: one},
        (1, 0): {1: one, 7: y, 8: z, 10: y * y + z * z},
        (1, 1): {7: one, 10: 2 * y},
        (1, 2): {10: one},
        (2, 0): {4: one, 11: y, 12: z},
        (2, 1): {11: one},
        (3, 0): {10: one},
    }
    table = np.zeros((len(BLOCKS) * LANES, ROWS))
    for place, block in enumerate(BLOCKS):
        for row, values in terms[block].items():
            table[place * LANES : (place + 1) * LANES, row] = values
    out = np.zeros((len(BLOCKS) * LANES, LANES), ml_dtypes.bfloat16)
    rest = table
    for part in range(3):
        piece = rest.astype(ml_dtypes.bfloat16)
        out[:, part * ROWS : (part + 1) * ROWS] = piece
        rest = rest - piece.astype(np.float64)
    return out


def field_rows(m, xi):
    rho = m[0]
    ux, uy, uz = m[1] / rho, m[2] / rho, m[3] / rho
    work = m[4] + m[5] + m[6]
    norm = ux * ux + uy * uy + uz * uz
    temp = (work / rho - norm) / 3.0
    along = ux * m[1] + uy * m[2] + uz * m[3]

    def heat(third, first, stress, u):
        return 0.5 * (
            third
            - 2.0 * (ux * stress[0] + uy * stress[1] + uz * stress[2])
            - u * work
            + norm * first
            + 2.0 * u * along
            - u * norm * rho
        )

    xheat = heat(m[10], m[1], (m[4], m[7], m[8]), ux)
    yheat = heat(m[11], m[2], (m[7], m[5], m[9]), uy)
    zheat = heat(m[12], m[3], (m[8], m[9], m[6]), uz)
    pressure = rho * temp
    conduct = (1.0 - diffusivity_ratio) / (5.0 * pressure * temp)
    root = jnp.sqrt(temp)
    amp = rho / (temp * root)
    retain = jnp.exp(-encounter_rate * rho * jnp.sqrt(root))
    inv = 1.0 / temp
    drift = xi - ux
    energy = drift * drift * inv
    height = (amp * (1.0 - retain)) * jnp.exp(-0.5 * energy)
    return height, energy - 5.0, drift * (conduct * xheat), [
        uy, uz, inv, conduct * yheat, conduct * zheat, retain,
    ]


def kernel(
    layers, cells, levels, spaces, vels,
    x_ref, w_ref, o_ref,
    stage, g_ref, r_ref, halo, sums, lhs, part, gathered, tall, wide, table, table_halo,
    splat, splat_halo,
    in_sem, out_sem, halo_send, halo_recv, tab_send, tab_recv, red_send, red_recv,
):
    f32 = jnp.float32
    s = lax.axis_index("space")
    v = lax.axis_index("vel")
    has_up = s < spaces - 1
    has_down = s > 0
    every = layers * cells
    nx = 2 * levels

    edge = 2
    spans = [(0, edge), (layers - edge, edge), (edge, layers - 2 * edge)]
    groups = [spans[:2], spans[2:]]
    starts = [0, 2 * edge * cells]
    sizes = [sum(n for _, n in group) * cells for group in groups]
    loads = []
    for i, (first, count) in enumerate(spans):
        rows = pl.ds(first * cells, count * cells)
        copy = pltpu.make_async_copy(x_ref.at[rows], stage.at[rows], in_sem.at[i])
        copy.start()
        loads.append(copy)

    barrier = pltpu.get_barrier_semaphore()
    for off in range(1, vels):
        pl.semaphore_signal(barrier, inc=1, device_id={"vel": lax.rem(v + off, vels)}, device_id_type=MESH)

    @pl.when(has_up)
    def _():
        pl.semaphore_signal(barrier, inc=1, device_id={"space": s + 1}, device_id_type=MESH)

    @pl.when(has_down)
    def _():
        pl.semaphore_signal(barrier, inc=1, device_id={"space": s - 1}, device_id_type=MESH)

    sub = lax.broadcasted_iota(jnp.int32, (SUB, LANES), 0)
    lane = lax.broadcasted_iota(jnp.int32, (SUB, LANES), 1)
    yv = -speed_limit + ((sub * PER_LANES + lane // NV).astype(f32) + 0.5) * SPACING
    zv = -speed_limit + ((lane % NV).astype(f32) + 0.5) * SPACING
    first_level = v * levels

    def speed(a):
        return ((first_level + a).astype(f32) + 0.5) * SPACING

    place = lax.broadcasted_iota(jnp.int32, (nx, LANES), 0)
    ahead = place >= levels
    level = jnp.where(ahead, place - levels, place) + first_level
    xi = jnp.where(ahead, 1.0, -1.0) * ((level.astype(f32) + 0.5) * SPACING)

    def sweep_coefs(speeds):
        n = COURANT_RATIO * jnp.abs(speeds)
        near = n * (2.0 - n)
        return near, 1.0 - n, jnp.where(speeds > 0.0, -near, near)

    ycoefs = sweep_coefs(yv)
    zcoefs = sweep_coefs(zv)

    def unpack(half, first, count):
        def body(i, _):
            for a in range(levels):
                g_ref[0, half, a, first + i // cells, i % cells] = stage[
                    first * cells + i, pl.ds(a * 2 * SUB + half, SUB, stride=2), :
                ]
            return 0

        lax.fori_loop(0, count * cells, body, 0, unroll=4)

    def stage_one(which, first, count):
        squares = []
        speeds = []
        for a in range(levels):
            xa = speed(jnp.int32(a))
            speeds.append(xa)
            squares.append(xa * xa)

        def body(i, _):
            layer = first + i // cells
            cell = i % cells
            total = [None] * 4
            for a in range(levels):
                back = g_ref[which, 0, a, layer, cell]
                fore = g_ref[which, 1, a, layer, cell]
                even = fore + back
                odd = (fore - back) * speeds[a]
                terms = [even, odd, even * squares[a], odd * squares[a]]
                total = [t if o is None else o + t for o, t in zip(total, terms)]
            at = (layer * cells + cell) * SUB
            for m in range(4):
                sums[m, pl.ds(at, SUB), :] = total[m]
            return 0

        lax.fori_loop(0, count * cells, body, 0, unroll=4)

    def stage_two(first, count, row):
        heights = [2.0 * SPACING * (PER_LANES / 4) * (2 * j - (SUB - 1)) for j in range(SUB)]

        def body(i, _):
            at = first * cells + i * SUB
            to = pl.multiple_of(row + i * SUB, SUB)
            for m, powers in enumerate((4, 3, 2, 1)):
                rows = [sums[m, pl.ds(at * SUB + j, SUB, stride=SUB), :] for j in range(SUB)]
                total = [None] * powers
                for j in range(SUB // 2):
                    low, high = rows[j], rows[SUB - 1 - j]
                    size = heights[SUB - 1 - j]
                    even = high + low
                    odd = (high - low) * size if powers > 1 else None
                    terms = [even, odd]
                    if powers > 2:
                        terms.append(even * (size * size))
                    if powers > 3:
                        terms.append(odd * (size * size))
                    total = [t if o is None else o + t for o, t in zip(total, terms[:powers])]
                for p in range(powers):
                    q = BLOCKS.index((m, p))
                    lhs[pl.ds(to, SUB), q * LANES : (q + 1) * LANES] = total[p]
            return 0

        lax.fori_loop(0, count * cells // SUB, body, 0, unroll=2)

    def reduce_copy(k, which, off):
        return pltpu.make_async_remote_copy(
            src_ref=part.at[k, which],
            dst_ref=gathered.at[k, which, off - 1],
            send_sem=red_send.at[k, which, off - 1],
            recv_sem=red_recv.at[k, which, off - 1],
            device_id={"vel": lax.rem(v + off, vels)},
            device_id_type=MESH,
        )

    def table_copy(k, half):
        first = edge * cells if half else 0
        return pltpu.make_async_remote_copy(
            src_ref=table.at[k, 0, pl.ds(first, edge * cells)],
            dst_ref=table_halo.at[k, half],
            send_sem=tab_send.at[k, half],
            recv_sem=tab_recv.at[k, half],
            device_id={"space": s + 1 if half else s - 1},
            device_id_type=MESH,
        )

    def halo_copy(k, half):
        first = layers - edge if half else 0
        return pltpu.make_async_remote_copy(
            src_ref=g_ref.at[k % 2, half, :, pl.ds(first, edge)],
            dst_ref=halo.at[k, half],
            send_sem=halo_send.at[k, half],
            recv_sem=halo_recv.at[k, half],
            device_id={"space": s + 1 if half else s - 1},
            device_id_type=MESH,
        )

    sends = {0: has_down, 1: has_up}
    receives = {0: has_up, 1: has_down}

    def moments(k, which):
        row = starts[which]
        for first, count in groups[which]:
            stage_two(first, count, row)
            row += count * cells
        size = sizes[which]
        rest = lhs[starts[which] : starts[which] + size, :]
        acc = None
        for _ in range(3):
            piece = rest.astype(jnp.bfloat16)
            term = jnp.dot(piece, w_ref[...], preferred_element_type=f32)
            acc = term if acc is None else acc + term
            rest = rest - piece.astype(f32)
        tall[0:size, :] = acc
        turned = tall[...].T
        part[k, which] = (
            turned[0:ROWS] + turned[ROWS : 2 * ROWS] + turned[2 * ROWS : 3 * ROWS]
        ) * QUADRATURE
        for off in range(1, vels):
            reduce_copy(k, which, off).start()

    def fill(source, target, rows, start):
        def body(i, _):
            at = pl.multiple_of(i * SUB, SUB)
            block = source[pl.ds(at, SUB), :]
            to = pl.multiple_of(start + i * SUB, SUB)
            for c in range(3 * nx + 6):
                target[c, pl.ds(to, SUB), :] = jnp.broadcast_to(block[:, c : c + 1], (SUB, LANES))
            return 0

        lax.fori_loop(0, rows // SUB, body, 0)

    def fields(k, which):
        total = part[k, which]
        for off in range(1, vels):
            reduce_copy(k, which, off).wait_recv()
            total = total + gathered[k, which, off - 1]
        m = [total[i : i + 1, :] for i in range(13)]
        height, energy, heat, rest = field_rows(m, xi)
        wide[0:nx, :] = height
        wide[nx : 2 * nx, :] = energy
        wide[2 * nx : 3 * nx, :] = heat
        for i, row in enumerate(rest):
            wide[3 * nx + i : 3 * nx + i + 1, :] = row
        table[k, which] = wide[...].T
        if which == 0:
            for half in range(2):
                @pl.when(sends[half])
                def _():
                    table_copy(k, half).start()
        fill(table.at[k, which], splat, sizes[which], starts[which])

    def relax_cell(source, row, halves, load, store):
        def spread(i):
            return source[i, pl.ds(row, 1), :]

        uy, uz, inv, qy, qz, retain = [spread(3 * nx + i) for i in range(6)]
        cy = yv - uy
        cz = zv - uz
        energy = (cy * cy + cz * cz) * inv
        heat = cy * qy + cz * qz
        gauss = jnp.exp(-0.5 * energy)
        for half in halves:
            for a in range(levels):
                i = half * levels + a
                bracket = 1.0 + (spread(2 * nx + i) + heat) * (spread(nx + i) + energy)
                store(half, a, (spread(i) * gauss) * bracket + load(half, a) * retain)

    def relax_own(k, first, count, row):
        def body(i, _):
            layer = first + i // cells
            cell = i % cells

            def load(half, a):
                return g_ref[k % 2, half, a, layer, cell]

            def store(half, a, value):
                r_ref[half, a, layer + edge * half, cell] = value

            relax_cell(splat, row + i, (0, 1), load, store)
            return 0

        lax.fori_loop(0, count * cells, body, 0, unroll=2)

    def relax_group(k, which):
        fields(k, which)
        row = starts[which]
        for first, count in groups[which]:
            relax_own(k, first, count, row)
            row += count * cells

    def relax_halo(k, half):
        def body(i, _):
            layer = i // cells
            cell = i % cells

            def load(half, a):
                return halo[k, half, a, layer, cell]

            def store(half, a, value):
                r_ref[half, a, layer + (0 if half else layers), cell] = value

            relax_cell(splat_halo, i, (half,), load, store)
            return 0

        fill(table_halo.at[k, half], splat_halo, edge * cells, 0)
        lax.fori_loop(0, edge * cells, body, 0, unroll=2)

    def periodic(values, coefs):
        near, keep, turn = coefs
        even, odd = values[0] + values[2], values[1] + values[3]
        deven, dodd = values[0] - values[2], values[1] - values[3]
        shift = near * (odd - even)
        e, o = even + shift, odd - shift
        de = keep * deven + turn * dodd
        do = keep * dodd - turn * deven
        return [e + de, o + do, e - de, o - do]

    def transport(k, half, first, count):
        last = k == STEPS - 1

        def body(i, _):
            a = i // count
            layer = first + i % count
            n = COURANT_RATIO * speed(a)
            own = 0.25 * (1.0 - n) * (1.0 - 0.5 * n)
            near = 0.25 * n * (2.0 - n)
            far = 0.125 * n * (n - 1.0)
            back = (2, 1, 0) if half else (0, 1, 2)
            moved = []
            for c in range(cells):
                r0, r1, r2 = [r_ref[half, a, layer + b, c] for b in back]
                moved.append(own * r0 + near * r1 + far * r2)
            for z in range(4):
                moved[z::4] = periodic(moved[z::4], ycoefs)
            for y in range(4):
                moved[4 * y : 4 * y + 4] = periodic(moved[4 * y : 4 * y + 4], zcoefs)
            for c in range(cells):
                if last:
                    stage[layer * cells + c, pl.ds(a * 2 * SUB + half, SUB, stride=2), :] = moved[c]
                else:
                    g_ref[(k + 1) % 2, half, a, layer, c] = moved[c]
            return 0

        lax.fori_loop(0, levels * count, body, 0, unroll=2)

    for half in range(2):
        @pl.when(jnp.logical_not(receives[half]))
        def _():
            for a in range(levels):
                for layer in range(edge):
                    r_ref[half, a, layer + (0 if half else layers)] = jnp.zeros((cells, SUB, LANES), f32)

    wide[...] = jnp.zeros_like(wide)
    tall[...] = jnp.zeros_like(tall)

    loads[0].wait()
    unpack(0, 0, edge)
    loads[1].wait()
    unpack(1, layers - edge, edge)

    greeted = vels - 1 + jnp.minimum(s, 1) + jnp.minimum(spaces - 1 - s, 1)
    pl.semaphore_wait(barrier, greeted)

    for half in range(2):
        @pl.when(sends[half])
        def _():
            halo_copy(0, half).start()

    unpack(1, 0, edge)
    unpack(0, layers - edge, edge)
    stage_one(0, 0, edge)
    stage_one(0, layers - edge, edge)
    moments(0, 0)
    loads[2].wait()
    unpack(0, edge, layers - 2 * edge)
    unpack(1, edge, layers - 2 * edge)
    stage_one(0, edge, layers - 2 * edge)
    moments(0, 1)

    stores = []

    def store_out(i):
        first, count = spans[i]
        rows = pl.ds(first * cells, count * cells)
        copy = pltpu.make_async_copy(stage.at[rows], o_ref.at[rows], out_sem.at[i])
        copy.start()
        stores.append(copy)

    for k in range(STEPS):
        last = k == STEPS - 1
        for which in (0, 1) if k == 0 else (1, 0):
            relax_group(k, which)
        transport(k, 1, layers - edge, edge)
        transport(k, 0, 0, edge)
        if not last:
            for half in range(2):
                @pl.when(sends[half])
                def _():
                    halo_copy(k + 1, half).start()
        for half in range(2):
            transport(k, half, edge, layers - 2 * edge)
        if last:
            store_out(2)
        else:
            stage_one((k + 1) % 2, edge, layers - 2 * edge)
            moments(k + 1, 1)
        for half in range(2):
            @pl.when(receives[half])
            def _():
                table_copy(k, half).wait_recv()
                halo_copy(k, half).wait_recv()
                relax_halo(k, half)

            transport(k, half, 0 if half else layers - edge, edge)
            span = 0 if half else 1
            if last:
                store_out(span)
            else:
                stage_one((k + 1) % 2, spans[span][0], edge)
        if not last:
            moments(k + 1, 0)
        for half in range(2):
            @pl.when(sends[half])
            def _():
                table_copy(k, half).wait_send()
                halo_copy(k, half).wait_send()
        for which in range(2):
            for off in range(1, vels):
                reduce_copy(k, which, off).wait_send()

    for copy in stores:
        copy.wait()


def local(distribution, weights, spaces, vels):
    layers, breadth, height, halves, velocities = distribution.shape
    cells = breadth * height
    assert breadth == 4 and height == 4 and halves == 2
    assert layers > 4 and (layers - 4) * cells <= LANES
    levels = velocities // (NV * NV)
    tiles = velocities // LANES
    every = layers * cells
    rows = distribution.reshape(every, halves, tiles, LANES)
    rows = rows.transpose(0, 2, 1, 3).reshape(every, tiles * halves, LANES)
    f32 = jnp.float32
    dma = pltpu.SemaphoreType.DMA
    out = pl.pallas_call(
        functools.partial(kernel, layers, cells, levels, spaces, vels),
        out_shape=jax.ShapeDtypeStruct(rows.shape, f32),
        in_specs=[
            pl.BlockSpec(memory_space=pl.ANY),
            pl.BlockSpec(memory_space=pltpu.VMEM),
        ],
        out_specs=pl.BlockSpec(memory_space=pl.ANY),
        scratch_shapes=[
            pltpu.VMEM(rows.shape, f32),
            pltpu.VMEM((2, 2, levels, layers, cells, SUB, LANES), f32),
            pltpu.VMEM((2, levels, layers + 2, cells, SUB, LANES), f32),
            pltpu.VMEM((STEPS, 2, levels, 2, cells, SUB, LANES), f32),
            pltpu.VMEM((4, every * SUB, LANES), f32),
            pltpu.VMEM((every, len(BLOCKS) * LANES), f32),
            pltpu.VMEM((STEPS, 2, ROWS, LANES), f32),
            pltpu.VMEM((STEPS, 2, max(vels - 1, 1), ROWS, LANES), f32),
            pltpu.VMEM((LANES, LANES), f32),
            pltpu.VMEM((LANES, LANES), f32),
            pltpu.VMEM((STEPS, 2, LANES, LANES), f32),
            pltpu.VMEM((STEPS, 2, 2 * cells, LANES), f32),
            pltpu.VMEM((6 * levels + 6, every, LANES), f32),
            pltpu.VMEM((6 * levels + 6, 2 * cells, LANES), f32),
            dma((3,)),
            dma((3,)),
            dma((STEPS, 2)),
            dma((STEPS, 2)),
            dma((STEPS, 2)),
            dma((STEPS, 2)),
            dma((STEPS, 2, max(vels - 1, 1))),
            dma((STEPS, 2, max(vels - 1, 1))),
        ],
        compiler_params=pltpu.CompilerParams(
            collective_id=0, has_side_effects=True, vmem_limit_bytes=48 * 2**20
        ),
    )(rows, weights)
    out = out.reshape(every, tiles, halves, LANES).transpose(0, 2, 1, 3)
    return out.reshape(distribution.shape)


def solution(mesh):
    weights = moment_table()
    spec = P("space", None, None, None, "vel")
    body = functools.partial(local, spaces=mesh.shape["space"], vels=mesh.shape["vel"])
    mapped = jax.shard_map(
        body, mesh=mesh, in_specs=(spec, P()), out_specs=spec, check_vma=False
    )
    return lambda distribution: mapped(distribution, jnp.asarray(weights))
```

```python
import functools
import math

import jax
import jax.numpy as jnp
import ml_dtypes
import numpy as np
from jax import lax
from jax.experimental import pallas as pl
from jax.experimental.pallas import tpu as pltpu
from jax.sharding import PartitionSpec as P

NV = 32
STEPS = 3
SUB = 8
LANES = 128

speed_limit = 8.0
courant = 1.9
diffusivity_ratio = 2.0 / 3.0
encounter_rate = 0.7

SPACING = 2.0 * speed_limit / NV
QUADRATURE = SPACING**3 / (2.0 * math.pi) ** 1.5
COURANT_RATIO = courant / ((NV - 1) * speed_limit / NV)
PER_LANES = LANES // NV
MESH = pl.DeviceIdType.MESH
BLOCKS = [(0, 0), (0, 1), (0, 2), (0, 3), (1, 0), (1, 1), (1, 2), (2, 0), (2, 1), (3, 0)]
ROWS = 16


def moment_table():
    lane = np.arange(LANES)
    y = SPACING * (lane // NV - 0.5 * (PER_LANES - 1))
    z = -speed_limit + (lane % NV + 0.5) * SPACING
    one = np.ones(LANES)
    terms = {
        (0, 0): {0: one, 2: y, 3: z, 5: y * y, 6: z * z, 9: y * z, 11: y**3 + y * z * z, 12: z * y * y + z**3},
        (0, 1): {2: one, 5: 2 * y, 9: z, 11: 3 * y * y + z * z, 12: 2 * y * z},
        (0, 2): {5: one, 11: 3 * y, 12: z},
        (0, 3): {11: one},
        (1, 0): {1: one, 7: y, 8: z, 10: y * y + z * z},
        (1, 1): {7: one, 10: 2 * y},
        (1, 2): {10: one},
        (2, 0): {4: one, 11: y, 12: z},
        (2, 1): {11: one},
        (3, 0): {10: one},
    }
    table = np.zeros((len(BLOCKS) * LANES, ROWS))
    for place, block in enumerate(BLOCKS):
        for row, values in terms[block].items():
            table[place * LANES : (place + 1) * LANES, row] = values
    out = np.zeros((len(BLOCKS) * LANES, LANES), ml_dtypes.bfloat16)
    rest = table
    for part in range(3):
        piece = rest.astype(ml_dtypes.bfloat16)
        out[:, part * ROWS : (part + 1) * ROWS] = piece
        rest = rest - piece.astype(np.float64)
    return out


def field_rows(m, xi):
    rho = m[0]
    ux, uy, uz = m[1] / rho, m[2] / rho, m[3] / rho
    work = m[4] + m[5] + m[6]
    norm = ux * ux + uy * uy + uz * uz
    temp = (work / rho - norm) / 3.0
    along = ux * m[1] + uy * m[2] + uz * m[3]

    def heat(third, first, stress, u):
        return 0.5 * (
            third
            - 2.0 * (ux * stress[0] + uy * stress[1] + uz * stress[2])
            - u * work
            + norm * first
            + 2.0 * u * along
            - u * norm * rho
        )

    xheat = heat(m[10], m[1], (m[4], m[7], m[8]), ux)
    yheat = heat(m[11], m[2], (m[7], m[5], m[9]), uy)
    zheat = heat(m[12], m[3], (m[8], m[9], m[6]), uz)
    pressure = rho * temp
    conduct = (1.0 - diffusivity_ratio) / (5.0 * pressure * temp)
    root = jnp.sqrt(temp)
    amp = rho / (temp * root)
    retain = jnp.exp(-encounter_rate * rho * jnp.sqrt(root))
    inv = 1.0 / temp
    drift = xi - ux
    energy = drift * drift * inv
    height = (amp * (1.0 - retain)) * jnp.exp(-0.5 * energy)
    return height, energy - 5.0, drift * (conduct * xheat), [
        uy, uz, inv, conduct * yheat, conduct * zheat, retain,
    ]


def kernel(
    layers, cells, levels, spaces, vels,
    x_ref, w_ref, o_ref,
    stage, g_ref, r_ref, halo, sums, lhs, part, gathered, tall, wide, table, table_halo,
    splat, splat_halo,
    in_sem, halo_send, halo_recv, tab_send, tab_recv, red_send, red_recv,
):
    f32 = jnp.float32
    s = lax.axis_index("space")
    v = lax.axis_index("vel")
    has_up = s < spaces - 1
    has_down = s > 0
    every = layers * cells
    nx = 2 * levels

    edge = 2
    spans = [(0, edge), (layers - edge, edge), (edge, layers - 2 * edge)]
    groups = [spans[:2], spans[2:]]
    starts = [0, 2 * edge * cells]
    sizes = [sum(n for _, n in group) * cells for group in groups]
    loads = []
    for i, (first, count) in enumerate(spans):
        rows = pl.ds(first * cells, count * cells)
        copy = pltpu.make_async_copy(x_ref.at[rows], stage.at[rows], in_sem.at[i])
        copy.start()
        loads.append(copy)

    barrier = pltpu.get_barrier_semaphore()
    for off in range(1, vels):
        pl.semaphore_signal(barrier, inc=1, device_id={"vel": lax.rem(v + off, vels)}, device_id_type=MESH)

    @pl.when(has_up)
    def _():
        pl.semaphore_signal(barrier, inc=1, device_id={"space": s + 1}, device_id_type=MESH)

    @pl.when(has_down)
    def _():
        pl.semaphore_signal(barrier, inc=1, device_id={"space": s - 1}, device_id_type=MESH)

    sub = lax.broadcasted_iota(jnp.int32, (SUB, LANES), 0)
    lane = lax.broadcasted_iota(jnp.int32, (SUB, LANES), 1)
    yv = -speed_limit + ((sub * PER_LANES + lane // NV).astype(f32) + 0.5) * SPACING
    zv = -speed_limit + ((lane % NV).astype(f32) + 0.5) * SPACING
    first_level = v * levels

    def speed(a):
        return ((first_level + a).astype(f32) + 0.5) * SPACING

    place = lax.broadcasted_iota(jnp.int32, (nx, LANES), 0)
    ahead = place >= levels
    level = jnp.where(ahead, place - levels, place) + first_level
    xi = jnp.where(ahead, 1.0, -1.0) * ((level.astype(f32) + 0.5) * SPACING)

    def sweep_coefs(speeds):
        n = COURANT_RATIO * jnp.abs(speeds)
        near = n * (2.0 - n)
        return near, 1.0 - n, jnp.where(speeds > 0.0, -near, near)

    ycoefs = sweep_coefs(yv)
    zcoefs = sweep_coefs(zv)

    def unpack(half, first, count):
        def body(i, _):
            for a in range(levels):
                g_ref[0, half, a, first + i // cells, i % cells] = stage[
                    first * cells + i, pl.ds(a * 2 * SUB + half, SUB, stride=2), :
                ]
            return 0

        lax.fori_loop(0, count * cells, body, 0, unroll=4)

    def stage_one(which, first, count):
        squares = []
        speeds = []
        for a in range(levels):
            xa = speed(jnp.int32(a))
            speeds.append(xa)
            squares.append(xa * xa)

        def body(i, _):
            layer = first + i // cells
            cell = i % cells
            total = [None] * 4
            for a in range(levels):
                back = g_ref[which, 0, a, layer, cell]
                fore = g_ref[which, 1, a, layer, cell]
                even = fore + back
                odd = (fore - back) * speeds[a]
                terms = [even, odd, even * squares[a], odd * squares[a]]
                total = [t if o is None else o + t for o, t in zip(total, terms)]
            at = (layer * cells + cell) * SUB
            for m in range(4):
                sums[m, pl.ds(at, SUB), :] = total[m]
            return 0

        lax.fori_loop(0, count * cells, body, 0, unroll=4)

    def stage_two(first, count, row):
        heights = [2.0 * SPACING * (PER_LANES / 4) * (2 * j - (SUB - 1)) for j in range(SUB)]

        def body(i, _):
            at = first * cells + i * SUB
            to = pl.multiple_of(row + i * SUB, SUB)
            for m, powers in enumerate((4, 3, 2, 1)):
                rows = [sums[m, pl.ds(at * SUB + j, SUB, stride=SUB), :] for j in range(SUB)]
                total = [None] * powers
                for j in range(SUB // 2):
                    low, high = rows[j], rows[SUB - 1 - j]
                    size = heights[SUB - 1 - j]
                    even = high + low
                    odd = (high - low) * size if powers > 1 else None
                    terms = [even, odd]
                    if powers > 2:
                        terms.append(even * (size * size))
                    if powers > 3:
                        terms.append(odd * (size * size))
                    total = [t if o is None else o + t for o, t in zip(total, terms[:powers])]
                for p in range(powers):
                    q = BLOCKS.index((m, p))
                    lhs[pl.ds(to, SUB), q * LANES : (q + 1) * LANES] = total[p]
            return 0

        lax.fori_loop(0, count * cells // SUB, body, 0, unroll=2)

    def reduce_copy(k, which, off):
        return pltpu.make_async_remote_copy(
            src_ref=part.at[k, which],
            dst_ref=gathered.at[k, which, off - 1],
            send_sem=red_send.at[k, which, off - 1],
            recv_sem=red_recv.at[k, which, off - 1],
            device_id={"vel": lax.rem(v + off, vels)},
            device_id_type=MESH,
        )

    def table_copy(k, half):
        first = edge * cells if half else 0
        return pltpu.make_async_remote_copy(
            src_ref=table.at[k, 0, pl.ds(first, edge * cells)],
            dst_ref=table_halo.at[k, half],
            send_sem=tab_send.at[k, half],
            recv_sem=tab_recv.at[k, half],
            device_id={"space": s + 1 if half else s - 1},
            device_id_type=MESH,
        )

    def halo_copy(k, half):
        first = layers - edge if half else 0
        return pltpu.make_async_remote_copy(
            src_ref=g_ref.at[k % 2, half, :, pl.ds(first, edge)],
            dst_ref=halo.at[k, half],
            send_sem=halo_send.at[k, half],
            recv_sem=halo_recv.at[k, half],
            device_id={"space": s + 1 if half else s - 1},
            device_id_type=MESH,
        )

    sends = {0: has_down, 1: has_up}
    receives = {0: has_up, 1: has_down}

    def moments(k, which):
        row = starts[which]
        for first, count in groups[which]:
            stage_two(first, count, row)
            row += count * cells
        size = sizes[which]
        rest = lhs[starts[which] : starts[which] + size, :]
        pieces = []
        for _ in range(3):
            pieces.append(rest.astype(jnp.bfloat16))
            rest = rest - pieces[-1].astype(f32)
        product = jnp.dot(jnp.concatenate(pieces, axis=0), w_ref[...], preferred_element_type=f32)
        tall[0:size, :] = product[0:size] + product[size : 2 * size] + product[2 * size : 3 * size]
        turned = tall[...].T
        part[k, which] = (
            turned[0:ROWS] + turned[ROWS : 2 * ROWS] + turned[2 * ROWS : 3 * ROWS]
        ) * QUADRATURE
        for off in range(1, vels):
            reduce_copy(k, which, off).start()

    def fill(source, target, rows, start):
        def body(i, _):
            at = pl.multiple_of(i * SUB, SUB)
            block = source[pl.ds(at, SUB), :]
            to = pl.multiple_of(start + i * SUB, SUB)
            for c in range(3 * nx + 6):
                target[c, pl.ds(to, SUB), :] = jnp.broadcast_to(block[:, c : c + 1], (SUB, LANES))
            return 0

        lax.fori_loop(0, rows // SUB, body, 0, unroll=4)

    def fields(k, which):
        total = part[k, which]
        for off in range(1, vels):
            reduce_copy(k, which, off).wait_recv()
            total = total + gathered[k, which, off - 1]
        m = [total[i : i + 1, :] for i in range(13)]
        height, energy, heat, rest = field_rows(m, xi)
        wide[0:nx, :] = height
        wide[nx : 2 * nx, :] = energy
        wide[2 * nx : 3 * nx, :] = heat
        for i, row in enumerate(rest):
            wide[3 * nx + i : 3 * nx + i + 1, :] = row
        table[k, which] = wide[...].T
        if which == 0:
            for half in range(2):
                @pl.when(sends[half])
                def _():
                    table_copy(k, half).start()
        fill(table.at[k, which], splat, sizes[which], starts[which])

    def relax_cell(source, row, halves, load, store):
        def spread(i):
            return source[i, pl.ds(row, 1), :]

        uy, uz, inv, qy, qz, retain = [spread(3 * nx + i) for i in range(6)]
        cy = yv - uy
        cz = zv - uz
        energy = (cy * cy + cz * cz) * inv
        heat = cy * qy + cz * qz
        gauss = jnp.exp(-0.5 * energy)
        for half in halves:
            for a in range(levels):
                i = half * levels + a
                bracket = 1.0 + (spread(2 * nx + i) + heat) * (spread(nx + i) + energy)
                store(half, a, (spread(i) * gauss) * bracket + load(half, a) * retain)

    def relax_own(k, first, count, row):
        def body(i, _):
            layer = first + i // cells
            cell = i % cells

            def load(half, a):
                return g_ref[k % 2, half, a, layer, cell]

            def store(half, a, value):
                r_ref[half, a, layer + edge * half, cell] = value

            relax_cell(splat, row + i, (0, 1), load, store)
            return 0

        lax.fori_loop(0, count * cells, body, 0, unroll=2)

    def relax_group(k, which):
        fields(k, which)
        row = starts[which]
        for first, count in groups[which]:
            relax_own(k, first, count, row)
            row += count * cells

    def relax_halo(k, half):
        def body(i, _):
            layer = i // cells
            cell = i % cells

            def load(half, a):
                return halo[k, half, a, layer, cell]

            def store(half, a, value):
                r_ref[half, a, layer + (0 if half else layers), cell] = value

            relax_cell(splat_halo, i, (half,), load, store)
            return 0

        fill(table_halo.at[k, half], splat_halo, edge * cells, 0)
        lax.fori_loop(0, edge * cells, body, 0, unroll=2)

    def periodic(values, coefs):
        near, keep, turn = coefs
        even, odd = values[0] + values[2], values[1] + values[3]
        deven, dodd = values[0] - values[2], values[1] - values[3]
        shift = near * (odd - even)
        e, o = even + shift, odd - shift
        de = keep * deven + turn * dodd
        do = keep * dodd - turn * deven
        return [e + de, o + do, e - de, o - do]

    def transport(k, half, first, count):
        last = k == STEPS - 1

        def body(i, _):
            a = i // count
            layer = first + i % count
            n = COURANT_RATIO * speed(a)
            own = 0.25 * (1.0 - n) * (1.0 - 0.5 * n)
            near = 0.25 * n * (2.0 - n)
            far = 0.125 * n * (n - 1.0)
            back = (2, 1, 0) if half else (0, 1, 2)
            moved = []
            for c in range(cells):
                r0, r1, r2 = [r_ref[half, a, layer + b, c] for b in back]
                moved.append(own * r0 + near * r1 + far * r2)
            for z in range(4):
                moved[z::4] = periodic(moved[z::4], ycoefs)
            for y in range(4):
                moved[4 * y : 4 * y + 4] = periodic(moved[4 * y : 4 * y + 4], zcoefs)
            for c in range(cells):
                if last:
                    o_ref[layer * cells + c, pl.ds(a * 2 * SUB + half, SUB, stride=2), :] = moved[c]
                else:
                    g_ref[(k + 1) % 2, half, a, layer, c] = moved[c]
            return 0

        lax.fori_loop(0, levels * count, body, 0, unroll=2)

    for half in range(2):
        @pl.when(jnp.logical_not(receives[half]))
        def _():
            for a in range(levels):
                for layer in range(edge):
                    r_ref[half, a, layer + (0 if half else layers)] = jnp.zeros((cells, SUB, LANES), f32)

    wide[...] = jnp.zeros_like(wide)
    tall[...] = jnp.zeros_like(tall)

    loads[0].wait()
    unpack(0, 0, edge)
    loads[1].wait()
    unpack(1, layers - edge, edge)

    greeted = vels - 1 + jnp.minimum(s, 1) + jnp.minimum(spaces - 1 - s, 1)
    pl.semaphore_wait(barrier, greeted)

    for half in range(2):
        @pl.when(sends[half])
        def _():
            halo_copy(0, half).start()

    unpack(1, 0, edge)
    unpack(0, layers - edge, edge)
    stage_one(0, 0, edge)
    stage_one(0, layers - edge, edge)
    moments(0, 0)
    loads[2].wait()
    unpack(0, edge, layers - 2 * edge)
    unpack(1, edge, layers - 2 * edge)
    stage_one(0, edge, layers - 2 * edge)
    moments(0, 1)

    for k in range(STEPS):
        last = k == STEPS - 1
        for which in (0, 1) if k == 0 else (1, 0):
            relax_group(k, which)
        transport(k, 1, layers - edge, edge)
        transport(k, 0, 0, edge)
        if not last:
            for half in range(2):
                @pl.when(sends[half])
                def _():
                    halo_copy(k + 1, half).start()
        for half in range(2):
            transport(k, half, edge, layers - 2 * edge)
        if not last:
            stage_one((k + 1) % 2, edge, layers - 2 * edge)
            moments(k + 1, 1)
        for half in range(2):
            @pl.when(receives[half])
            def _():
                table_copy(k, half).wait_recv()
                halo_copy(k, half).wait_recv()
                relax_halo(k, half)

            transport(k, half, 0 if half else layers - edge, edge)
            span = 0 if half else 1
            if not last:
                stage_one((k + 1) % 2, spans[span][0], edge)
        if not last:
            moments(k + 1, 0)
        for half in range(2):
            @pl.when(sends[half])
            def _():
                table_copy(k, half).wait_send()
                halo_copy(k, half).wait_send()
        for which in range(2):
            for off in range(1, vels):
                reduce_copy(k, which, off).wait_send()


def local(distribution, weights, spaces, vels):
    layers, breadth, height, halves, velocities = distribution.shape
    cells = breadth * height
    assert breadth == 4 and height == 4 and halves == 2
    assert layers > 4 and (layers - 4) * cells <= LANES
    levels = velocities // (NV * NV)
    tiles = velocities // LANES
    every = layers * cells
    rows = distribution.reshape(every, halves, tiles, LANES)
    rows = rows.transpose(0, 2, 1, 3).reshape(every, tiles * halves, LANES)
    f32 = jnp.float32
    dma = pltpu.SemaphoreType.DMA
    out = pl.pallas_call(
        functools.partial(kernel, layers, cells, levels, spaces, vels),
        out_shape=jax.ShapeDtypeStruct(rows.shape, f32),
        in_specs=[
            pl.BlockSpec(memory_space=pl.ANY),
            pl.BlockSpec(memory_space=pltpu.VMEM),
        ],
        out_specs=pl.BlockSpec(memory_space=pltpu.VMEM),
        scratch_shapes=[
            pltpu.VMEM(rows.shape, f32),
            pltpu.VMEM((2, 2, levels, layers, cells, SUB, LANES), f32),
            pltpu.VMEM((2, levels, layers + 2, cells, SUB, LANES), f32),
            pltpu.VMEM((STEPS, 2, levels, 2, cells, SUB, LANES), f32),
            pltpu.VMEM((4, every * SUB, LANES), f32),
            pltpu.VMEM((every, len(BLOCKS) * LANES), f32),
            pltpu.VMEM((STEPS, 2, ROWS, LANES), f32),
            pltpu.VMEM((STEPS, 2, max(vels - 1, 1), ROWS, LANES), f32),
            pltpu.VMEM((LANES, LANES), f32),
            pltpu.VMEM((LANES, LANES), f32),
            pltpu.VMEM((STEPS, 2, LANES, LANES), f32),
            pltpu.VMEM((STEPS, 2, 2 * cells, LANES), f32),
            pltpu.VMEM((6 * levels + 6, every, LANES), f32),
            pltpu.VMEM((6 * levels + 6, 2 * cells, LANES), f32),
            dma((3,)),
            dma((STEPS, 2)),
            dma((STEPS, 2)),
            dma((STEPS, 2)),
            dma((STEPS, 2)),
            dma((STEPS, 2, max(vels - 1, 1))),
            dma((STEPS, 2, max(vels - 1, 1))),
        ],
        compiler_params=pltpu.CompilerParams(
            collective_id=0, has_side_effects=True, vmem_limit_bytes=48 * 2**20
        ),
    )(rows, weights)
    out = out.reshape(every, tiles, halves, LANES).transpose(0, 2, 1, 3)
    return out.reshape(distribution.shape)


def solution(mesh):
    weights = moment_table()
    spec = P("space", None, None, None, "vel")
    body = functools.partial(local, spaces=mesh.shape["space"], vels=mesh.shape["vel"])
    mapped = jax.shard_map(
        body, mesh=mesh, in_specs=(spec, P()), out_specs=spec, check_vma=False
    )
    return lambda distribution: mapped(distribution, jnp.asarray(weights))
```
